32 devices in a mesh: grp: 2 (over core), dom: 16 (over z, y, x).
Axes of the slice: x: 2, y: 2, z: 4, core: 2. Of those that a mesh axis runs over, the one named last changes fastest.
Arguments:
- reduced_basis: bfloat16 [98304, 256], P(('grp', 'dom')), may hold values from -6 to 6
- tangents: bfloat16 [4096, 4096], P(('grp', 'dom')), may hold values from -1 to 2, as said below
- connectivity: int32 [20, 4096], P(None, ('grp', 'dom')), may hold values from 0 to 1151, as said below
- weights: float32 [4096], P(('grp', 'dom')), may hold values from 0.5 to 8
Outputs:
- residual_basis: bfloat16 [98304, 256], P(('grp', 'dom'))
- galerkin_tangent: float32 [256, 256], replicated
- lspg_tangent: float32 [256, 256], replicated
The draws below stay inside these ranges and needn't reach their ends.
Inputs may be any that keep to these rules, and one draw needn't show every extreme that they name: `connectivity`: numbers below 1024 are the partition's own nodes; 1024 + k is node k of the next partition in grp+dom order; the last partition names only its own nodes. An element's node numbers lie in a range of 64, except that a partition's first element may also name node 0 and its last element node 1151. `tangents`: each tangent is symmetric, and its rows and columns 60 to 63 are zero.
All inputs are finite; a program needn't handle non-finite values.
Results may differ from the reference program's by a relative error of at most 0.0013.
Values may be sent and summed in bfloat16 or wider, within the bound.
A program may use at most 64 MiB of HBM per device.

```python
import math
import jax
import jax.numpy as jnp
from jax import lax

R = 256
NPE = 20
EDOF = 64
NODE_DEV = 1024
ELEMS = 128
RIM = 128
SPAN = 64
NDOF = 98304
ELEMS_ALL = 4096
N_GRP = 2
N_DOM = 16


def draw_tangents(key, part):
    devices = ELEMS_ALL // ELEMS
    active = 3 * NPE

    def one_block(position):
        block_key = jax.random.fold_in(jax.random.fold_in(key, 7001), position)
        first_key, second_key = jax.random.split(block_key)
        raw = 0.35 * jax.random.normal(first_key, (ELEMS, active, active), jnp.float32)
        symmetric = 0.5 * (raw + jnp.swapaxes(raw, 1, 2))
        diagonal = jax.random.uniform(second_key, (ELEMS, active), jnp.float32, 6.0, 9.0)
        full = (symmetric + diagonal[:, :, None] * jnp.eye(active, dtype=jnp.float32)[None]) / 8.0
        full = jnp.pad(full, ((0, 0), (0, EDOF - active), (0, EDOF - active)))
        return full.reshape(ELEMS, EDOF * EDOF).astype(jnp.bfloat16)
    blocks = lax.map(one_block, jnp.arange(devices, dtype=jnp.int32))
    return blocks.reshape(ELEMS_ALL, EDOF * EDOF)


def draw_connectivity(key, part):
    devices = ELEMS_ALL // ELEMS
    first_key, second_key = jax.random.split(jax.random.fold_in(key, 7002))
    element_index = jnp.arange(ELEMS_ALL, dtype=jnp.int32)
    owner = element_index // ELEMS
    top_base = jnp.where(owner == devices - 1, NODE_DEV - SPAN, NODE_DEV + RIM - SPAN)
    base_nodes = jax.random.randint(first_key, (ELEMS_ALL,), 0, 1 << 30, dtype=jnp.int32) % (top_base + 1)
    offsets = jax.random.randint(second_key, (NPE, ELEMS_ALL), 0, SPAN, dtype=jnp.int32)
    nodes = base_nodes[None, :] + offsets
    is_first = element_index % ELEMS == 0
    is_final = (element_index % ELEMS == ELEMS - 1) & (owner < devices - 1)
    nodes = nodes.at[0].set(jnp.where(is_first, 0, nodes[0]))
    nodes = nodes.at[NPE - 1].set(jnp.where(is_final, NODE_DEV + RIM - 1, nodes[NPE - 1]))
    return nodes.astype(jnp.int32)


def strengthened(drawn, rng, source, target, parts, factor):
    def block_of(dim):
        return (jnp.arange(drawn.shape[dim]) // (drawn.shape[dim] // parts)).reshape((-1,) + (1,) * (drawn.ndim - 1 - dim))

    near = jax.random.permutation(rng, parts)[block_of(target)]
    far = (block_of(target) + parts // 2) % parts
    return jnp.where((block_of(source) == near) | (block_of(source) == far), factor * drawn, drawn)


def block_levels(rng, shape, pieces, smallest, high):
    gain = 1.0
    for axis_at, shards_of in pieces:
        draws = jax.random.uniform(jax.random.fold_in(jax.random.fold_in(rng, 6), axis_at), (shards_of,), jnp.float32, smallest / len(pieces), high / len(pieces))
        gain = gain * jnp.repeat(jnp.exp(draws), shape[axis_at] // shards_of).reshape((-1,) + (1,) * (len(shape) - 1 - axis_at))
    return gain


def bell_draw_with(rng, extent, deviation, limit, pieces, heavy, held_as=jnp.bfloat16):
    array = deviation * jax.random.normal(rng, extent, jnp.float32)
    if pieces:
        array = array * block_levels(rng, extent, pieces, -0.22, 0.18)
    return jnp.clip(strengthened(array, jax.random.fold_in(rng, 3), *heavy), -limit, limit).astype(held_as)


def setup_inputs(seed: int = 0) -> dict:
    keys = jax.random.split(jax.random.key(seed), 5)
    reduced_basis = bell_draw_with(keys[0], (NDOF, R), 1.0, 6.0, ((0, 32),), (0, 1, 32, 2.75))
    tangents = draw_tangents(jax.random.fold_in(keys[4], 71), 0)
    connectivity = draw_connectivity(jax.random.fold_in(keys[4], 71), 0)
    weights = jnp.clip(jnp.exp(math.log(8.0) - 2.7725887 * jax.random.uniform(keys[3], (ELEMS_ALL,), jnp.float32) ** block_levels(keys[3], (ELEMS_ALL,), ((0, 32),), -0.2, 0.2)), 0.5, 8.0)
    return dict(reduced_basis=reduced_basis, tangents=tangents, connectivity=connectivity, weights=weights)


def element_rows(nodes):
    triples = nodes.T[:, :, None] * 3 + jnp.arange(3, dtype=jnp.int32)[None, None, :]
    flattened = triples.reshape(nodes.shape[1], -1).astype(jnp.int32)
    padding = jnp.zeros((nodes.shape[1], EDOF - flattened.shape[1]), jnp.int32)
    return jnp.concatenate([flattened, padding], axis=1)


def reference(reduced_basis, tangents, connectivity, weights):
    devices = N_GRP * N_DOM
    own_rows = NODE_DEV * 3
    rim_rows = RIM * 3
    padded = jnp.concatenate([reduced_basis, jnp.zeros((rim_rows, R), reduced_basis.dtype)], axis=0)
    tangent_blocks = tangents.reshape(devices, ELEMS, EDOF, EDOF)
    node_blocks = jnp.transpose(connectivity.reshape(NPE, devices, ELEMS), (1, 0, 2))
    weight_blocks = weights.reshape(devices, ELEMS)

    def partition(carry, inputs):
        tangent_set, node_set, weight_set, position = inputs
        extended = lax.dynamic_slice_in_dim(padded, (position * own_rows).astype(jnp.int32), own_rows + rim_rows, 0)
        dof_rows = element_rows(node_set)
        gathered = extended[dof_rows].astype(jnp.float32)
        products = jnp.einsum("eij,ejc->eic", tangent_set.astype(jnp.float32), gathered, precision=lax.Precision.HIGHEST)
        scaled = products * weight_set[:, None, None]
        assembled = jnp.zeros((own_rows + rim_rows, R), jnp.float32).at[dof_rows.reshape(-1)].add(scaled.reshape(-1, R))
        owned = assembled[:own_rows].at[:rim_rows].add(carry)
        residual_rows = owned.astype(jnp.bfloat16)
        basis_rows = extended[:own_rows].astype(jnp.float32)
        wide_rows = residual_rows.astype(jnp.float32)
        galerkin_part = jnp.einsum("rc,rd->cd", basis_rows, wide_rows, precision=lax.Precision.HIGHEST)
        lspg_part = jnp.einsum("rc,rd->cd", wide_rows, wide_rows, precision=lax.Precision.HIGHEST)
        return assembled[own_rows:], (residual_rows, galerkin_part, lspg_part)

    positions = jnp.arange(devices, dtype=jnp.int32)
    start_rim = jnp.zeros((rim_rows, R), jnp.float32)
    final_rim, outputs = lax.scan(partition, start_rim, (tangent_blocks, node_blocks, weight_blocks, positions))
    rows_all, galerkin_parts, lspg_parts = outputs
    scale_factor = 1.0 / float(NDOF)
    galerkin_tangent = jnp.sum(galerkin_parts, axis=0) * scale_factor
    lspg_tangent = jnp.sum(lspg_parts, axis=0) * scale_factor
    return (rows_all.reshape(NDOF, R), galerkin_tangent, lspg_tangent)
```

```python
import functools

import jax
import jax.numpy as jnp
from jax import lax
from jax.experimental import pallas as pl
from jax.experimental.pallas import tpu as pltpu
from jax.sharding import PartitionSpec as P

EDOF = 64
RIM = 128
LANES = 128
GROUP = 4
MESH = pl.DeviceIdType.MESH
VMEM_LIMIT = 48 * 1024 * 1024


def passed_along(x, axis, by):
    peers = lax.axis_size(axis)
    pairs = [(i, i + by) for i in range(peers) if 0 <= i + by < peers]
    return lax.ppermute(x, axis, pairs)


def transposed_dot(left, right):
    return lax.dot_general(
        left, right, (((0,), (0,)), ((), ())), preferred_element_type=jnp.float32
    )


def assemble_kernel(
    own_rows, rim_rows, nodes_ref, weights_ref, basis_ref, rim_ref, tangents_ref,
    rows_ref, edge_ref, over_ref, *scratch,
):
    halves = basis_ref.shape[1] // LANES
    table = scratch[:halves]
    totals = [scratch[halves * (1 + u):halves * (2 + u)] for u in range(GROUP)]
    at = halves * (1 + GROUP)
    picked = [scratch[at + halves * u:at + halves * (u + 1)] for u in range(GROUP)]
    at += halves * GROUP
    products = [scratch[at + halves * u:at + halves * (u + 1)] for u in range(GROUP)]
    node_count, elem_count = nodes_ref.shape
    chunk = rim_rows
    all_rows = own_rows + rim_rows

    def widen(i, carry):
        at_rows = pl.ds(pl.multiple_of(i * chunk, chunk), chunk)
        for h in range(halves):
            table[h][at_rows, :] = basis_ref[at_rows, h * LANES:(h + 1) * LANES].astype(jnp.float32)
            for u in range(GROUP):
                totals[u][h][at_rows, :] = jnp.zeros((chunk, LANES), jnp.float32)
        return carry

    lax.fori_loop(0, own_rows // chunk, widen, 0)
    for h in range(halves):
        table[h][own_rows:all_rows, :] = rim_ref[:, h * LANES:(h + 1) * LANES].astype(jnp.float32)
        table[h][all_rows:all_rows + 8, :] = jnp.zeros((8, LANES), jnp.float32)
        for u in range(GROUP):
            totals[u][h][own_rows:all_rows + 8, :] = jnp.zeros((rim_rows + 8, LANES), jnp.float32)
    keep = lax.broadcasted_iota(jnp.int32, (8, LANES), 0) < 3

    def add_group(i, carry):
        base = i * GROUP
        starts = [[nodes_ref[k, base + u] * 3 for k in range(node_count)] for u in range(GROUP)]
        for u in range(GROUP):
            for k in range(node_count):
                for h in range(halves):
                    picked[u][h][3 * k:3 * k + 8, :] = table[h][pl.ds(starts[u][k], 8), :]
        for u in range(GROUP):
            block = jnp.concatenate([picked[u][h][:EDOF, :] for h in range(halves)], axis=1)
            product = jnp.dot(
                tangents_ref[base + u], block.astype(jnp.bfloat16),
                preferred_element_type=jnp.float32,
            ) * weights_ref[base + u]
            for h in range(halves):
                products[u][h][:EDOF, :] = product[:, h * LANES:(h + 1) * LANES]
        for k in range(node_count):
            for u in range(GROUP):
                for h in range(halves):
                    part = jnp.where(keep, products[u][h][3 * k:3 * k + 8, :], 0.0)
                    spot = pl.ds(starts[u][k], 8)
                    totals[u][h][spot, :] = totals[u][h][spot, :] + part
        return carry

    for u in range(GROUP):
        for h in range(halves):
            picked[u][h][...] = jnp.zeros(picked[u][h].shape, jnp.float32)
            products[u][h][...] = jnp.zeros(products[u][h].shape, jnp.float32)
    lax.fori_loop(0, elem_count // GROUP, add_group, 0)

    def summed(at_rows, h):
        value = totals[0][h][at_rows, :]
        for u in range(1, GROUP):
            value = value + totals[u][h][at_rows, :]
        return value

    def finish(i, carry):
        at_rows = pl.ds(pl.multiple_of(i * chunk, chunk), chunk)
        for h in range(halves):
            rows_ref[at_rows, h * LANES:(h + 1) * LANES] = summed(at_rows, h).astype(jnp.bfloat16)
        return carry

    lax.fori_loop(1, own_rows // chunk, finish, 0)
    for h in range(halves):
        lanes = slice(h * LANES, (h + 1) * LANES)
        edge = summed(pl.ds(0, rim_rows), h)
        edge_ref[:, lanes] = edge
        rows_ref[0:rim_rows, lanes] = edge.astype(jnp.bfloat16)
        over_ref[:, lanes] = summed(pl.ds(own_rows, rim_rows), h)


def assemble(basis, rim_basis, tangents, nodes, weights):
    own_rows, columns = basis.shape
    rim_rows = rim_basis.shape[0]
    halves = columns // LANES
    tall = pltpu.VMEM((own_rows + rim_rows + 8, LANES), jnp.float32)
    short = pltpu.VMEM((EDOF + 8, LANES), jnp.float32)
    vmem = pl.BlockSpec(memory_space=pltpu.VMEM)
    smem = pl.BlockSpec(memory_space=pltpu.SMEM)
    return pl.pallas_call(
        functools.partial(assemble_kernel, own_rows, rim_rows),
        out_shape=(
            jax.ShapeDtypeStruct((own_rows, columns), jnp.bfloat16),
            jax.ShapeDtypeStruct((rim_rows, columns), jnp.float32),
            jax.ShapeDtypeStruct((rim_rows, columns), jnp.float32),
        ),
        in_specs=[smem, smem, vmem, vmem, vmem],
        out_specs=(vmem, vmem, vmem),
        scratch_shapes=[tall] * (halves * (1 + GROUP)) + [short] * (halves * GROUP * 2),
        compiler_params=pltpu.CompilerParams(vmem_limit_bytes=VMEM_LIMIT),
        name="assemble",
    )(nodes, weights, basis, rim_basis, tangents)


def reduce_kernel(
    peers, factor, basis_ref, rows_ref, edge_ref, over_ref, out_ref, edge_out_ref,
    arrived, part, half, shards, mine, rim_sems, pair_sems, send_sems, recv_sems,
    spread_sems, spread_recv, pass_sems, pass_recv,
):
    g = lax.axis_index("grp")
    d = lax.axis_index("dom")
    sibling = (1 - g, d)
    rim_rows, columns = edge_ref.shape
    own_rows = basis_ref.shape[0]
    height = columns // peers
    spot = g * peers + d
    after = lax.rem(spot + 1, 2 * peers)
    before = lax.rem(spot + 2 * peers - 1, 2 * peers)
    following = (after // peers, lax.rem(after, peers))
    previous = (before // peers, lax.rem(before, peers))

    def shard(of):
        return pl.ds(pl.multiple_of(of * height, height), height)

    def peer(k):
        return lax.rem(d + k, peers)

    barrier = pltpu.get_barrier_semaphore()
    greeted = [sibling, following, previous] + [(g, peer(k)) for k in range(1, peers)]
    for device in greeted:
        pl.semaphore_signal(barrier, inc=1, device_id=device, device_id_type=MESH)
    pl.semaphore_wait(barrier, len(greeted))

    def remote(src, dst, send, recv, device):
        return pltpu.make_async_remote_copy(
            src_ref=src, dst_ref=dst, send_sem=send, recv_sem=recv,
            device_id=device, device_id_type=MESH,
        )

    rim_copy = remote(over_ref, arrived, rim_sems.at[0], rim_sems.at[1], following)
    rim_copy.start()
    part[...] = jnp.zeros(part.shape, jnp.float32)

    def project(i, carry):
        at_rows = pl.ds(pl.multiple_of(i * rim_rows, rim_rows), rim_rows)
        rows = rows_ref[at_rows, :]
        part[0] += transposed_dot(basis_ref[at_rows, :], rows)
        part[1] += transposed_dot(rows, rows)
        return carry

    lax.fori_loop(1, own_rows // rim_rows, project, 0)
    rim_copy.wait()
    edge_rows = (edge_ref[...] + arrived[...]).astype(jnp.bfloat16)
    edge_out_ref[...] = edge_rows
    part[0] += transposed_dot(basis_ref[0:rim_rows, :], edge_rows)
    part[1] += transposed_dot(edge_rows, edge_rows)

    pair_copy = remote(part.at[1 - g], half, pair_sems.at[0], pair_sems.at[1], sibling)
    pair_copy.start()
    pair_copy.wait()
    half[...] = half[...] + part[g]

    copies = []
    for k in range(1, peers):
        copy = remote(
            half.at[shard(peer(k))], shards.at[k], send_sems.at[k], recv_sems.at[k], (g, peer(k))
        )
        copy.start()
        copies.append(copy)
    total = half[shard(d), :]
    for k in range(1, peers):
        copies[k - 1].wait_recv()
        total = total + shards[k]
    mine[...] = total * factor
    for copy in copies:
        copy.wait_send()

    spreads = []
    for k in range(1, peers):
        copy = remote(
            mine, out_ref.at[g, shard(d)], spread_sems.at[k], spread_recv.at[k], (g, peer(k))
        )
        copy.start()
        spreads.append(copy)
    passes = []
    own = remote(mine, out_ref.at[g, shard(d)], pass_sems.at[0], pass_recv.at[0], sibling)
    own.start()
    passes.append(own)
    out_ref[g, shard(d), :] = mine[...]
    for k in range(1, peers):
        spreads[k - 1].wait_recv()
        source = lax.rem(d + peers - k, peers)
        place = out_ref.at[g, shard(source)]
        copy = remote(place, place, pass_sems.at[k], pass_recv.at[k], sibling)
        copy.start()
        passes.append(copy)
    for copy in spreads:
        copy.wait_send()
    for copy in passes:
        copy.wait()


def reduce_all(basis, rows, edge, over, peers, factor):
    rim_rows, columns = edge.shape
    height = columns // peers
    vmem = pl.BlockSpec(memory_space=pltpu.VMEM)
    dma = pltpu.SemaphoreType.DMA
    return pl.pallas_call(
        functools.partial(reduce_kernel, peers, factor),
        out_shape=(
            jax.ShapeDtypeStruct((2, columns, columns), jnp.float32),
            jax.ShapeDtypeStruct((rim_rows, columns), jnp.bfloat16),
        ),
        in_specs=[vmem] * 4,
        out_specs=(vmem, vmem),
        scratch_shapes=[
            pltpu.VMEM((rim_rows, columns), jnp.float32),
            pltpu.VMEM((2, columns, columns), jnp.float32),
            pltpu.VMEM((columns, columns), jnp.float32),
            pltpu.VMEM((peers, height, columns), jnp.float32),
            pltpu.VMEM((height, columns), jnp.float32),
            dma((2,)), dma((2,)), dma((peers,)), dma((peers,)),
            dma((peers,)), dma((peers,)), dma((peers,)), dma((peers,)),
        ],
        compiler_params=pltpu.CompilerParams(
            collective_id=0, has_side_effects=True, vmem_limit_bytes=VMEM_LIMIT
        ),
        name="reduce_all",
    )(basis, rows, edge, over)


def local(reduced_basis, tangents, connectivity, weights):
    own_rows, columns = reduced_basis.shape
    rim_rows = RIM * 3
    elem_count = weights.shape[0]
    groups, peers = lax.axis_size("grp"), lax.axis_size("dom")
    factor = 1.0 / float(own_rows * groups * peers)
    rim_basis = passed_along(reduced_basis[:rim_rows], ("grp", "dom"), -1)
    rows, edge, over = assemble(
        reduced_basis, rim_basis, tangents.reshape(elem_count, EDOF, EDOF), connectivity, weights
    )
    if groups == 2 and columns % peers == 0 and (columns // peers) % 8 == 0:
        both, edge_rows = reduce_all(reduced_basis, rows, edge, over, peers, factor)
        return lax.dynamic_update_slice(rows, edge_rows, (0, 0)), both[0], both[1]
    incoming = passed_along(over, ("grp", "dom"), 1)
    edge_rows = (edge + incoming).astype(jnp.bfloat16)
    rows = lax.dynamic_update_slice(rows, edge_rows, (0, 0))
    sums = lax.psum(
        (transposed_dot(reduced_basis, rows), transposed_dot(rows, rows)), ("grp", "dom")
    )
    return rows, sums[0] * factor, sums[1] * factor


def solution(mesh):
    placed = (
        P(("grp", "dom"), None),
        P(("grp", "dom"), None),
        P(None, ("grp", "dom")),
        P(("grp", "dom")),
    )
    return jax.shard_map(
        local,
        mesh=mesh,
        in_specs=placed,
        out_specs=(P(("grp", "dom"), None), P(), P()),
        check_vma=False,
    )
```

```python
import functools

import jax
import jax.numpy as jnp
from jax import lax
from jax.experimental import pallas as pl
from jax.experimental.pallas import tpu as pltpu
from jax.sharding import PartitionSpec as P

EDOF = 64
RIM = 128
LANES = 128
GROUP = 4
MESH = pl.DeviceIdType.MESH
VMEM_LIMIT = 48 * 1024 * 1024


def passed_along(x, axis, by):
    peers = lax.axis_size(axis)
    pairs = [(i, i + by) for i in range(peers) if 0 <= i + by < peers]
    return lax.ppermute(x, axis, pairs)


def transposed_dot(left, right):
    return lax.dot_general(
        left, right, (((0,), (0,)), ((), ())), preferred_element_type=jnp.float32
    )


def ring_neighbours(g, d, groups, peers):
    spot = g * peers + d
    after = lax.rem(spot + 1, groups * peers)
    before = lax.rem(spot + groups * peers - 1, groups * peers)
    return (after // peers, lax.rem(after, peers)), (before // peers, lax.rem(before, peers))


def prepare_kernel(
    groups, peers, basis_ref, tangents_ref, rim_ref, laid_ref, flat, spread, sems
):
    g, d = lax.axis_index("grp"), lax.axis_index("dom")
    following, previous = ring_neighbours(g, d, groups, peers)
    rim_rows = rim_ref.shape[0]
    elems, width = flat.shape
    lines = width // LANES
    load = pltpu.make_async_copy(tangents_ref, flat, sems.at[0])
    load.start()
    barrier = pltpu.get_barrier_semaphore()
    for device in (following, previous):
        pl.semaphore_signal(barrier, inc=1, device_id=device, device_id_type=MESH)
    pl.semaphore_wait(barrier, 2)
    rim_copy = pltpu.make_async_remote_copy(
        src_ref=basis_ref.at[pl.ds(0, rim_rows)], dst_ref=rim_ref,
        send_sem=sems.at[1], recv_sem=sems.at[2], device_id=previous, device_id_type=MESH,
    )
    rim_copy.start()
    load.wait()
    for m in range(lines):
        block = flat[:, m * LANES:(m + 1) * LANES].astype(jnp.float32)
        spread[pl.ds(m, elems, stride=lines + 8), :] = block
    for e in range(elems):
        piece = spread[e * (lines + 8):e * (lines + 8) + lines, :]
        laid_ref[e * lines:(e + 1) * lines, :] = piece.astype(jnp.bfloat16)
    rim_copy.wait()


def prepare(basis, tangents, rim_rows, groups, peers):
    elems, width = tangents.shape
    columns = basis.shape[1]
    lines = width // LANES
    vmem = pl.BlockSpec(memory_space=pltpu.VMEM)
    whole = pl.BlockSpec(memory_space=pltpu.HBM)
    return pl.pallas_call(
        functools.partial(prepare_kernel, groups, peers),
        out_shape=(
            jax.ShapeDtypeStruct((rim_rows, columns), jnp.bfloat16),
            jax.ShapeDtypeStruct((elems * lines, LANES), jnp.bfloat16),
        ),
        in_specs=[whole, whole],
        out_specs=(vmem, vmem),
        scratch_shapes=[
            pltpu.VMEM((elems, width), jnp.bfloat16),
            pltpu.VMEM((elems * (lines + 8), LANES), jnp.float32),
            pltpu.SemaphoreType.DMA((3,)),
        ],
        compiler_params=pltpu.CompilerParams(
            collective_id=1, has_side_effects=True, vmem_limit_bytes=VMEM_LIMIT
        ),
        name="prepare",
    )(basis, tangents)


def assemble_kernel(
    own_rows, rim_rows, nodes_ref, weights_ref, basis_hbm, rim_ref, laid_ref,
    rows_ref, edge_ref, over_ref, basis_ref, basis_sem, *scratch,
):
    halves = basis_ref.shape[1] // LANES
    taken = iter(scratch)

    def buffers():
        return [next(taken) for _ in range(halves)]

    table = buffers()
    totals = [buffers() for _ in range(GROUP)]
    picked = [[buffers() for _ in range(GROUP)] for _ in range(2)]
    products = [[buffers() for _ in range(GROUP)] for _ in range(2)]
    node_count, elem_count = nodes_ref.shape
    lines = laid_ref.shape[0] // elem_count
    chunk = rim_rows
    all_rows = own_rows + rim_rows
    load = pltpu.make_async_copy(basis_hbm, basis_ref, basis_sem)
    load.start()

    def clear(i, carry):
        at_rows = pl.ds(pl.multiple_of(i * chunk, chunk), chunk)
        for h in range(halves):
            for u in range(GROUP):
                totals[u][h][at_rows, :] = jnp.zeros((chunk, LANES), jnp.float32)
        return carry

    lax.fori_loop(0, all_rows // chunk, clear, 0)
    for h in range(halves):
        table[h][own_rows:all_rows, :] = rim_ref[:, h * LANES:(h + 1) * LANES].astype(jnp.float32)
        table[h][all_rows:all_rows + 8, :] = jnp.zeros((8, LANES), jnp.float32)
        for u in range(GROUP):
            totals[u][h][all_rows:all_rows + 8, :] = jnp.zeros((8, LANES), jnp.float32)
            for turn in range(2):
                for buffer in (picked[turn][u][h], products[turn][u][h]):
                    buffer[...] = jnp.zeros(buffer.shape, jnp.float32)
    load.wait()

    def widen(i, carry):
        at_rows = pl.ds(pl.multiple_of(i * chunk, chunk), chunk)
        for h in range(halves):
            table[h][at_rows, :] = basis_ref[at_rows, h * LANES:(h + 1) * LANES].astype(jnp.float32)
        return carry

    lax.fori_loop(0, own_rows // chunk, widen, 0)
    keep = lax.broadcasted_iota(jnp.int32, (8, LANES), 0) < 3

    def scatter(turn, base):
        for k in range(node_count):
            for u in range(GROUP):
                spot = pl.ds(nodes_ref[k, base + u] * 3, 8)
                for h in range(halves):
                    part = jnp.where(keep, products[turn][u][h][3 * k:3 * k + 8, :], 0.0)
                    totals[u][h][spot, :] = totals[u][h][spot, :] + part

    def multiply(turn, base):
        for u in range(GROUP):
            for k in range(node_count):
                spot = pl.ds(nodes_ref[k, base + u] * 3, 8)
                for h in range(halves):
                    picked[turn][u][h][3 * k:3 * k + 8, :] = table[h][spot, :]
        for u in range(GROUP):
            block = jnp.concatenate([picked[turn][u][h][:EDOF, :] for h in range(halves)], axis=1)
            pairs = laid_ref[pl.ds(pl.multiple_of((base + u) * lines, lines), lines), :]
            matrix = jnp.concatenate([pairs[:, :EDOF], pairs[:, EDOF:]], axis=0)
            product = jnp.dot(
                matrix, block.astype(jnp.bfloat16), preferred_element_type=jnp.float32
            ) * weights_ref[base + u]
            for h in range(halves):
                lanes = slice(h * LANES, (h + 1) * LANES)
                products[turn][u][h][pl.ds(0, lines, stride=2), :] = product[:lines, lanes]
                products[turn][u][h][pl.ds(1, lines, stride=2), :] = product[lines:, lanes]

    def add_pair(i, carry):
        base = i * (2 * GROUP)
        multiply(0, base)
        scatter(1, jnp.maximum(base - GROUP, 0))
        multiply(1, base + GROUP)
        scatter(0, base)
        return carry

    lax.fori_loop(0, elem_count // (2 * GROUP), add_pair, 0)
    scatter(1, elem_count - GROUP)

    def summed(at_rows, h):
        value = totals[0][h][at_rows, :]
        for u in range(1, GROUP):
            value = value + totals[u][h][at_rows, :]
        return value

    def finish(i, carry):
        at_rows = pl.ds(pl.multiple_of(i * chunk, chunk), chunk)
        for h in range(halves):
            rows_ref[at_rows, h * LANES:(h + 1) * LANES] = summed(at_rows, h).astype(jnp.bfloat16)
        return carry

    lax.fori_loop(1, own_rows // chunk, finish, 0)
    for h in range(halves):
        lanes = slice(h * LANES, (h + 1) * LANES)
        edge = summed(pl.ds(0, rim_rows), h)
        edge_ref[:, lanes] = edge
        rows_ref[0:rim_rows, lanes] = edge.astype(jnp.bfloat16)
        over_ref[:, lanes] = summed(pl.ds(own_rows, rim_rows), h)


def assemble(basis, rim_basis, laid, nodes, weights):
    own_rows, columns = basis.shape
    rim_rows = rim_basis.shape[0]
    halves = columns // LANES
    tall = pltpu.VMEM((own_rows + rim_rows + 8, LANES), jnp.float32)
    short = pltpu.VMEM((EDOF + 8, LANES), jnp.float32)
    vmem = pl.BlockSpec(memory_space=pltpu.VMEM)
    smem = pl.BlockSpec(memory_space=pltpu.SMEM)
    whole = pl.BlockSpec(memory_space=pltpu.HBM)
    return pl.pallas_call(
        functools.partial(assemble_kernel, own_rows, rim_rows),
        out_shape=(
            jax.ShapeDtypeStruct((own_rows, columns), jnp.bfloat16),
            jax.ShapeDtypeStruct((rim_rows, columns), jnp.float32),
            jax.ShapeDtypeStruct((rim_rows, columns), jnp.float32),
        ),
        in_specs=[smem, smem, whole, vmem, vmem],
        out_specs=(vmem, vmem, vmem),
        scratch_shapes=[pltpu.VMEM((own_rows, columns), jnp.bfloat16), pltpu.SemaphoreType.DMA]
        + [tall] * (halves * (1 + GROUP)) + [short] * (halves * GROUP * 4),
        compiler_params=pltpu.CompilerParams(vmem_limit_bytes=VMEM_LIMIT),
        name="assemble",
    )(nodes, weights, basis, rim_basis, laid)


def reduce_kernel(
    peers, factor, basis_hbm, rows_hbm, edge_ref, over_ref, out_ref, edge_out_ref,
    basis_ref, rows_ref, load_sems, arrived, part, half, shards, mine, rim_sems, pair_sems, send_sems, recv_sems,
    spread_sems, spread_recv, pass_sems, pass_recv,
):
    g = lax.axis_index("grp")
    d = lax.axis_index("dom")
    sibling = (1 - g, d)
    rim_rows, columns = edge_ref.shape
    own_rows = basis_ref.shape[0]
    height = columns // peers
    following, previous = ring_neighbours(g, d, 2, peers)
    loads = [
        pltpu.make_async_copy(basis_hbm, basis_ref, load_sems.at[0]),
        pltpu.make_async_copy(rows_hbm, rows_ref, load_sems.at[1]),
    ]
    for load in loads:
        load.start()

    def shard(of):
        return pl.ds(pl.multiple_of(of * height, height), height)

    def peer(k):
        return lax.rem(d + k, peers)

    barrier = pltpu.get_barrier_semaphore()
    greeted = [sibling, following, previous] + [(g, peer(k)) for k in range(1, peers)]
    for device in greeted:
        pl.semaphore_signal(barrier, inc=1, device_id=device, device_id_type=MESH)
    pl.semaphore_wait(barrier, len(greeted))

    def remote(src, dst, send, recv, device):
        return pltpu.make_async_remote_copy(
            src_ref=src, dst_ref=dst, send_sem=send, recv_sem=recv,
            device_id=device, device_id_type=MESH,
        )

    rim_copy = remote(over_ref, arrived, rim_sems.at[0], rim_sems.at[1], following)
    rim_copy.start()
    part[...] = jnp.zeros(part.shape, jnp.float32)
    for load in loads:
        load.wait()

    def project(i, carry):
        at_rows = pl.ds(pl.multiple_of(i * rim_rows, rim_rows), rim_rows)
        rows = rows_ref[at_rows, :]
        part[0] += transposed_dot(basis_ref[at_rows, :], rows)
        part[1] += transposed_dot(rows, rows)
        return carry

    lax.fori_loop(1, own_rows // rim_rows, project, 0)
    rim_copy.wait()
    edge_rows = (edge_ref[...] + arrived[...]).astype(jnp.bfloat16)
    edge_out_ref[...] = edge_rows
    part[0] += transposed_dot(basis_ref[0:rim_rows, :], edge_rows)
    part[1] += transposed_dot(edge_rows, edge_rows)

    pair_copy = remote(part.at[1 - g], half, pair_sems.at[0], pair_sems.at[1], sibling)
    pair_copy.start()
    pair_copy.wait()
    half[...] = half[...] + part[g]

    copies = []
    for k in range(1, peers):
        copy = remote(
            half.at[shard(peer(k))], shards.at[k], send_sems.at[k], recv_sems.at[k], (g, peer(k))
        )
        copy.start()
        copies.append(copy)
    total = half[shard(d), :]
    for k in range(1, peers):
        copies[k - 1].wait_recv()
        total = total + shards[k]
    mine[...] = total * factor
    for copy in copies:
        copy.wait_send()

    spreads = []
    for k in range(1, peers):
        copy = remote(
            mine, out_ref.at[g, shard(d)], spread_sems.at[k], spread_recv.at[k], (g, peer(k))
        )
        copy.start()
        spreads.append(copy)
    passes = []
    own = remote(mine, out_ref.at[g, shard(d)], pass_sems.at[0], pass_recv.at[0], sibling)
    own.start()
    passes.append(own)
    out_ref[g, shard(d), :] = mine[...]
    for k in range(1, peers):
        spreads[k - 1].wait_recv()
        source = lax.rem(d + peers - k, peers)
        place = out_ref.at[g, shard(source)]
        copy = remote(place, place, pass_sems.at[k], pass_recv.at[k], sibling)
        copy.start()
        passes.append(copy)
    for copy in spreads:
        copy.wait_send()
    for copy in passes:
        copy.wait()


def reduce_all(basis, rows, edge, over, peers, factor):
    rim_rows, columns = edge.shape
    height = columns // peers
    vmem = pl.BlockSpec(memory_space=pltpu.VMEM)
    whole = pl.BlockSpec(memory_space=pltpu.HBM)
    dma = pltpu.SemaphoreType.DMA
    return pl.pallas_call(
        functools.partial(reduce_kernel, peers, factor),
        out_shape=(
            jax.ShapeDtypeStruct((2, columns, columns), jnp.float32),
            jax.ShapeDtypeStruct((rim_rows, columns), jnp.bfloat16),
        ),
        in_specs=[whole, whole, vmem, vmem],
        out_specs=(vmem, vmem),
        scratch_shapes=[
            pltpu.VMEM(basis.shape, jnp.bfloat16), pltpu.VMEM(rows.shape, jnp.bfloat16), dma((2,)),
            pltpu.VMEM((rim_rows, columns), jnp.float32),
            pltpu.VMEM((2, columns, columns), jnp.float32),
            pltpu.VMEM((columns, columns), jnp.float32),
            pltpu.VMEM((peers, height, columns), jnp.float32),
            pltpu.VMEM((height, columns), jnp.float32),
            dma((2,)), dma((2,)), dma((peers,)), dma((peers,)),
            dma((peers,)), dma((peers,)), dma((peers,)), dma((peers,)),
        ],
        compiler_params=pltpu.CompilerParams(
            collective_id=0, has_side_effects=True, vmem_limit_bytes=VMEM_LIMIT
        ),
        name="reduce_all",
    )(basis, rows, edge, over)


def local(reduced_basis, tangents, connectivity, weights):
    own_rows, columns = reduced_basis.shape
    rim_rows = RIM * 3
    groups, peers = lax.axis_size("grp"), lax.axis_size("dom")
    factor = 1.0 / float(own_rows * groups * peers)
    rim_basis, laid = prepare(reduced_basis, tangents, rim_rows, groups, peers)
    rows, edge, over = assemble(reduced_basis, rim_basis, laid, connectivity, weights)
    if groups == 2 and columns % peers == 0 and (columns // peers) % 8 == 0:
        both, edge_rows = reduce_all(reduced_basis, rows, edge, over, peers, factor)
        return lax.dynamic_update_slice(rows, edge_rows, (0, 0)), both[0], both[1]
    incoming = passed_along(over, ("grp", "dom"), 1)
    edge_rows = (edge + incoming).astype(jnp.bfloat16)
    rows = lax.dynamic_update_slice(rows, edge_rows, (0, 0))
    sums = lax.psum(
        (transposed_dot(reduced_basis, rows), transposed_dot(rows, rows)), ("grp", "dom")
    )
    return rows, sums[0] * factor, sums[1] * factor


def solution(mesh):
    placed = (
        P(("grp", "dom"), None),
        P(("grp", "dom"), None),
        P(None, ("grp", "dom")),
        P(("grp", "dom")),
    )
    return jax.shard_map(
        local,
        mesh=mesh,
        in_specs=placed,
        out_specs=(P(("grp", "dom"), None), P(), P()),
        check_vma=False,
    )
```

```python
import functools

import jax
import jax.numpy as jnp
from jax import lax
from jax.experimental import pallas as pl
from jax.experimental.pallas import tpu as pltpu
from jax.sharding import PartitionSpec as P

EDOF = 64
RIM = 128
LANES = 128
GROUP = 4
RIM_TYPE = jnp.bfloat16
RIM_SCALE = 1.0
MESH = pl.DeviceIdType.MESH
VMEM_LIMIT = 60 * 1024 * 1024


def passed_along(x, axis, by):
    peers = lax.axis_size(axis)
    pairs = [(i, i + by) for i in range(peers) if 0 <= i + by < peers]
    return lax.ppermute(x, axis, pairs)


def transposed_dot(left, right):
    return lax.dot_general(
        left, right, (((0,), (0,)), ((), ())), preferred_element_type=jnp.float32
    )


def ring_neighbours(g, d, groups, peers):
    spot = g * peers + d
    after = lax.rem(spot + 1, groups * peers)
    before = lax.rem(spot + groups * peers - 1, groups * peers)
    following = (after // peers, lax.rem(after, peers))
    previous = (before // peers, lax.rem(before, peers))
    return spot, following, previous


def prepare_kernel(
    groups, peers, basis_ref, tangents_ref, rim_ref, laid_ref, flat, spread, sems
):
    g, d = lax.axis_index("grp"), lax.axis_index("dom")
    spot, following, previous = ring_neighbours(g, d, groups, peers)
    has_next, has_previous = spot < groups * peers - 1, spot > 0
    rim_rows = rim_ref.shape[0]
    elems, width = flat.shape
    lines = width // LANES
    load = pltpu.make_async_copy(tangents_ref, flat, sems.at[0])
    load.start()
    barrier = pltpu.get_barrier_semaphore()
    for present, device in ((has_next, following), (has_previous, previous)):
        @pl.when(present)
        def _(device=device):
            pl.semaphore_signal(barrier, inc=1, device_id=device, device_id_type=MESH)
    pl.semaphore_wait(barrier, has_next.astype(jnp.int32) + has_previous.astype(jnp.int32))
    rim_copy = pltpu.make_async_remote_copy(
        src_ref=basis_ref.at[pl.ds(0, rim_rows)], dst_ref=rim_ref,
        send_sem=sems.at[1], recv_sem=sems.at[2], device_id=previous, device_id_type=MESH,
    )
    pl.when(has_previous)(rim_copy.start)
    load.wait()
    for m in range(lines):
        block = flat[:, m * LANES:(m + 1) * LANES].astype(jnp.float32)
        spread[pl.ds(m, elems, stride=lines + 8), :] = block
    for e in range(elems):
        piece = spread[e * (lines + 8):e * (lines + 8) + lines, :]
        laid_ref[e * lines:(e + 1) * lines, :] = piece.astype(jnp.bfloat16)
    pl.when(has_next)(rim_copy.wait_recv)

    @pl.when(jnp.logical_not(has_next))
    def _():
        rim_ref[...] = jnp.zeros(rim_ref.shape, rim_ref.dtype)

    pl.when(has_previous)(rim_copy.wait_send)


def prepare(basis, tangents, rim_rows, groups, peers):
    elems, width = tangents.shape
    columns = basis.shape[1]
    lines = width // LANES
    vmem = pl.BlockSpec(memory_space=pltpu.VMEM)
    whole = pl.BlockSpec(memory_space=pltpu.HBM)
    return pl.pallas_call(
        functools.partial(prepare_kernel, groups, peers),
        out_shape=(
            jax.ShapeDtypeStruct((rim_rows, columns), jnp.bfloat16),
            jax.ShapeDtypeStruct((elems * lines, LANES), jnp.bfloat16),
        ),
        in_specs=[whole, whole],
        out_specs=(vmem, vmem),
        scratch_shapes=[
            pltpu.VMEM((elems, width), jnp.bfloat16),
            pltpu.VMEM((elems * (lines + 8), LANES), jnp.float32),
            pltpu.SemaphoreType.DMA((3,)),
        ],
        compiler_params=pltpu.CompilerParams(
            collective_id=1, has_side_effects=True, vmem_limit_bytes=VMEM_LIMIT
        ),
        name="prepare",
    )(basis, tangents)


def assemble_kernel(
    own_rows, rim_rows, nodes_ref, weights_ref, basis_hbm, rim_ref, laid_ref,
    rows_ref, edge_ref, over_ref, basis_ref, basis_sem, *scratch,
):
    halves = basis_ref.shape[1] // LANES
    taken = iter(scratch)

    def buffers():
        return [next(taken) for _ in range(halves)]

    table = buffers()
    totals = [buffers() for _ in range(GROUP)]
    picked = [[buffers() for _ in range(GROUP)] for _ in range(2)]
    products = [[buffers() for _ in range(GROUP)] for _ in range(2)]
    node_count, elem_count = nodes_ref.shape
    lines = laid_ref.shape[0] // elem_count
    chunk = rim_rows
    all_rows = own_rows + rim_rows
    load = pltpu.make_async_copy(basis_hbm, basis_ref, basis_sem)
    load.start()

    def clear(i, carry):
        at_rows = pl.ds(pl.multiple_of(i * chunk, chunk), chunk)
        for h in range(halves):
            for u in range(GROUP):
                totals[u][h][at_rows, :] = jnp.zeros((chunk, LANES), jnp.float32)
        return carry

    lax.fori_loop(0, all_rows // chunk, clear, 0)
    for h in range(halves):
        table[h][own_rows:all_rows, :] = rim_ref[:, h * LANES:(h + 1) * LANES].astype(jnp.float32)
        table[h][all_rows:all_rows + 8, :] = jnp.zeros((8, LANES), jnp.float32)
        for u in range(GROUP):
            totals[u][h][all_rows:all_rows + 8, :] = jnp.zeros((8, LANES), jnp.float32)
            for turn in range(2):
                for buffer in (picked[turn][u][h], products[turn][u][h]):
                    buffer[...] = jnp.zeros(buffer.shape, jnp.float32)
    load.wait()

    def widen(i, carry):
        at_rows = pl.ds(pl.multiple_of(i * chunk, chunk), chunk)
        for h in range(halves):
            table[h][at_rows, :] = basis_ref[at_rows, h * LANES:(h + 1) * LANES].astype(jnp.float32)
        return carry

    lax.fori_loop(0, own_rows // chunk, widen, 0)
    keep = lax.broadcasted_iota(jnp.int32, (8, LANES), 0) < 3

    def scatter(turn, base):
        for k in range(node_count):
            for u in range(GROUP):
                spot = pl.ds(nodes_ref[k, base + u] * 3, 8)
                for h in range(halves):
                    part = jnp.where(keep, products[turn][u][h][3 * k:3 * k + 8, :], 0.0)
                    totals[u][h][spot, :] = totals[u][h][spot, :] + part

    def multiply(turn, base):
        for u in range(GROUP):
            for k in range(node_count):
                spot = pl.ds(nodes_ref[k, base + u] * 3, 8)
                for h in range(halves):
                    picked[turn][u][h][3 * k:3 * k + 8, :] = table[h][spot, :]
        for u in range(GROUP):
            block = jnp.concatenate([picked[turn][u][h][:EDOF, :] for h in range(halves)], axis=1)
            pairs = laid_ref[pl.ds(pl.multiple_of((base + u) * lines, lines), lines), :]
            matrix = jnp.concatenate([pairs[:, :EDOF], pairs[:, EDOF:]], axis=0)
            product = jnp.dot(
                matrix, block.astype(jnp.bfloat16), preferred_element_type=jnp.float32
            ) * weights_ref[base + u]
            for h in range(halves):
                lanes = slice(h * LANES, (h + 1) * LANES)
                products[turn][u][h][pl.ds(0, lines, stride=2), :] = product[:lines, lanes]
                products[turn][u][h][pl.ds(1, lines, stride=2), :] = product[lines:, lanes]

    def add_pair(i, carry):
        base = i * (2 * GROUP)
        multiply(0, base)
        scatter(1, jnp.maximum(base - GROUP, 0))
        multiply(1, base + GROUP)
        scatter(0, base)
        return carry

    lax.fori_loop(0, elem_count // (2 * GROUP), add_pair, 0)
    scatter(1, elem_count - GROUP)

    def summed(at_rows, h):
        value = totals[0][h][at_rows, :]
        for u in range(1, GROUP):
            value = value + totals[u][h][at_rows, :]
        return value

    def finish(i, carry):
        at_rows = pl.ds(pl.multiple_of(i * chunk, chunk), chunk)
        for h in range(halves):
            rows_ref[at_rows, h * LANES:(h + 1) * LANES] = summed(at_rows, h).astype(jnp.bfloat16)
        return carry

    lax.fori_loop(1, own_rows // chunk, finish, 0)
    for h in range(halves):
        lanes = slice(h * LANES, (h + 1) * LANES)
        edge = summed(pl.ds(0, rim_rows), h)
        edge_ref[:, lanes] = edge
        rows_ref[0:rim_rows, lanes] = edge.astype(jnp.bfloat16)
        over = summed(pl.ds(own_rows, rim_rows), h)
        over_ref[:, lanes] = (over * (1.0 / RIM_SCALE)).astype(over_ref.dtype)


def assemble(basis, rim_basis, laid, nodes, weights):
    own_rows, columns = basis.shape
    rim_rows = rim_basis.shape[0]
    halves = columns // LANES
    tall = pltpu.VMEM((own_rows + rim_rows + 8, LANES), jnp.float32)
    short = pltpu.VMEM((EDOF + 8, LANES), jnp.float32)
    vmem = pl.BlockSpec(memory_space=pltpu.VMEM)
    smem = pl.BlockSpec(memory_space=pltpu.SMEM)
    whole = pl.BlockSpec(memory_space=pltpu.HBM)
    return pl.pallas_call(
        functools.partial(assemble_kernel, own_rows, rim_rows),
        out_shape=(
            jax.ShapeDtypeStruct((own_rows, columns), jnp.bfloat16),
            jax.ShapeDtypeStruct((rim_rows, columns), jnp.float32),
            jax.ShapeDtypeStruct((rim_rows, columns), RIM_TYPE),
        ),
        in_specs=[smem, smem, whole, vmem, vmem],
        out_specs=(vmem, vmem, vmem),
        scratch_shapes=[pltpu.VMEM((own_rows, columns), jnp.bfloat16), pltpu.SemaphoreType.DMA]
        + [tall] * (halves * (1 + GROUP)) + [short] * (halves * GROUP * 4),
        compiler_params=pltpu.CompilerParams(vmem_limit_bytes=VMEM_LIMIT),
        name="assemble",
    )(nodes, weights, basis, rim_basis, laid)


def reduce_kernel(
    peers, factor, basis_hbm, rows_hbm, edge_ref, over_ref, out_ref, edge_out_ref,
    basis_ref, rows_ref, load_sems, arrived, part, half, shards, mine, rim_sems, pair_sems, send_sems, recv_sems,
    spread_sems, spread_recv, pass_sems, pass_recv,
):
    g = lax.axis_index("grp")
    d = lax.axis_index("dom")
    sibling = (1 - g, d)
    rim_rows, columns = edge_ref.shape
    own_rows = basis_ref.shape[0]
    height = columns // peers
    spot, following, previous = ring_neighbours(g, d, 2, peers)
    has_next, has_previous = spot < 2 * peers - 1, spot > 0
    loads = [
        pltpu.make_async_copy(basis_hbm, basis_ref, load_sems.at[0]),
        pltpu.make_async_copy(rows_hbm, rows_ref, load_sems.at[1]),
    ]
    for load in loads:
        load.start()

    def shard(of):
        return pl.ds(pl.multiple_of(of * height, height), height)

    def peer(k):
        return lax.rem(d + k, peers)

    barrier = pltpu.get_barrier_semaphore()
    greeted = [sibling] + [(g, peer(k)) for k in range(1, peers)]
    for device in greeted:
        pl.semaphore_signal(barrier, inc=1, device_id=device, device_id_type=MESH)
    for present, device in ((has_next, following), (has_previous, previous)):
        @pl.when(present)
        def _(device=device):
            pl.semaphore_signal(barrier, inc=1, device_id=device, device_id_type=MESH)
    ring = has_next.astype(jnp.int32) + has_previous.astype(jnp.int32)
    pl.semaphore_wait(barrier, len(greeted) + ring)

    def remote(src, dst, send, recv, device):
        return pltpu.make_async_remote_copy(
            src_ref=src, dst_ref=dst, send_sem=send, recv_sem=recv,
            device_id=device, device_id_type=MESH,
        )

    rim_copy = remote(over_ref, arrived, rim_sems.at[0], rim_sems.at[1], following)
    pl.when(has_next)(rim_copy.start)
    part[...] = jnp.zeros(part.shape, jnp.float32)
    for load in loads:
        load.wait()

    def project(i, carry):
        at_rows = pl.ds(pl.multiple_of(i * rim_rows, rim_rows), rim_rows)
        rows = rows_ref[at_rows, :]
        part[0] += transposed_dot(basis_ref[at_rows, :], rows)
        part[1] += transposed_dot(rows, rows)
        return carry

    lax.fori_loop(1, own_rows // rim_rows, project, 0)
    pl.when(has_previous)(rim_copy.wait_recv)

    @pl.when(jnp.logical_not(has_previous))
    def _():
        arrived[...] = jnp.zeros(arrived.shape, arrived.dtype)

    incoming = arrived[...].astype(jnp.float32) * RIM_SCALE
    edge_rows = (edge_ref[...] + incoming).astype(jnp.bfloat16)
    edge_out_ref[...] = edge_rows
    part[0] += transposed_dot(basis_ref[0:rim_rows, :], edge_rows)
    part[1] += transposed_dot(edge_rows, edge_rows)

    pair_copy = remote(part.at[1 - g], half, pair_sems.at[0], pair_sems.at[1], sibling)
    pair_copy.start()
    pl.when(has_next)(rim_copy.wait_send)
    pair_copy.wait()
    half[...] = half[...] + part[g]

    copies = []
    for k in range(1, peers):
        copy = remote(
            half.at[shard(peer(k))], shards.at[k], send_sems.at[k], recv_sems.at[k], (g, peer(k))
        )
        copy.start()
        copies.append(copy)
    total = half[shard(d), :]
    for k in range(1, peers):
        copies[k - 1].wait_recv()
        total = total + shards[k]
    mine[...] = total * factor
    for copy in copies:
        copy.wait_send()

    spreads = []
    for k in range(1, peers):
        copy = remote(
            mine, out_ref.at[g, shard(d)], spread_sems.at[k], spread_recv.at[k], (g, peer(k))
        )
        copy.start()
        spreads.append(copy)
    passes = []
    own = remote(mine, out_ref.at[g, shard(d)], pass_sems.at[0], pass_recv.at[0], sibling)
    own.start()
    passes.append(own)
    out_ref[g, shard(d), :] = mine[...]
    for k in range(1, peers):
        spreads[k - 1].wait_recv()
        source = lax.rem(d + peers - k, peers)
        place = out_ref.at[g, shard(source)]
        copy = remote(place, place, pass_sems.at[k], pass_recv.at[k], sibling)
        copy.start()
        passes.append(copy)
    for copy in spreads:
        copy.wait_send()
    for copy in passes:
        copy.wait()


def reduce_all(basis, rows, edge, over, peers, factor):
    rim_rows, columns = edge.shape
    height = columns // peers
    vmem = pl.BlockSpec(memory_space=pltpu.VMEM)
    whole = pl.BlockSpec(memory_space=pltpu.HBM)
    dma = pltpu.SemaphoreType.DMA
    return pl.pallas_call(
        functools.partial(reduce_kernel, peers, factor),
        out_shape=(
            jax.ShapeDtypeStruct((2, columns, columns), jnp.float32),
            jax.ShapeDtypeStruct((rim_rows, columns), jnp.bfloat16),
        ),
        in_specs=[whole, whole, vmem, vmem],
        out_specs=(vmem, vmem),
        scratch_shapes=[
            pltpu.VMEM(basis.shape, jnp.bfloat16), pltpu.VMEM(rows.shape, jnp.bfloat16), dma((2,)),
            pltpu.VMEM((rim_rows, columns), RIM_TYPE),
            pltpu.VMEM((2, columns, columns), jnp.float32),
            pltpu.VMEM((columns, columns), jnp.float32),
            pltpu.VMEM((peers, height, columns), jnp.float32),
            pltpu.VMEM((height, columns), jnp.float32),
            dma((2,)), dma((2,)), dma((peers,)), dma((peers,)),
            dma((peers,)), dma((peers,)), dma((peers,)), dma((peers,)),
        ],
        compiler_params=pltpu.CompilerParams(
            collective_id=0, has_side_effects=True, vmem_limit_bytes=VMEM_LIMIT
        ),
        name="reduce_all",
    )(basis, rows, edge, over)


def local(reduced_basis, tangents, connectivity, weights):
    own_rows, columns = reduced_basis.shape
    rim_rows = RIM * 3
    groups, peers = lax.axis_size("grp"), lax.axis_size("dom")
    factor = 1.0 / float(own_rows * groups * peers)
    rim_basis, laid = prepare(reduced_basis, tangents, rim_rows, groups, peers)
    rows, edge, over = assemble(reduced_basis, rim_basis, laid, connectivity, weights)
    if groups == 2 and columns % peers == 0 and (columns // peers) % 8 == 0:
        both, edge_rows = reduce_all(reduced_basis, rows, edge, over, peers, factor)
        return lax.dynamic_update_slice(rows, edge_rows, (0, 0)), both[0], both[1]
    incoming = passed_along(over, ("grp", "dom"), 1).astype(jnp.float32) * RIM_SCALE
    edge_rows = (edge + incoming).astype(jnp.bfloat16)
    rows = lax.dynamic_update_slice(rows, edge_rows, (0, 0))
    sums = lax.psum(
        (transposed_dot(reduced_basis, rows), transposed_dot(rows, rows)), ("grp", "dom")
    )
    return rows, sums[0] * factor, sums[1] * factor


def solution(mesh):
    placed = (
        P(("grp", "dom"), None),
        P(("grp", "dom"), None),
        P(None, ("grp", "dom")),
        P(("grp", "dom")),
    )
    return jax.shard_map(
        local,
        mesh=mesh,
        in_specs=placed,
        out_specs=(P(("grp", "dom"), None), P(), P()),
        check_vma=False,
    )
```

```python
import functools

import jax
import jax.numpy as jnp
from jax import lax
from jax.experimental import pallas as pl
from jax.experimental.pallas import tpu as pltpu
from jax.sharding import PartitionSpec as P

EDOF = 64
RIM = 128
LANES = 128
GROUP = 4
RIM_TYPE = jnp.bfloat16
RIM_SCALE = 1.0
MESH = pl.DeviceIdType.MESH
VMEM_LIMIT = 60 * 1024 * 1024


def passed_along(x, axis, by):
    peers = lax.axis_size(axis)
    pairs = [(i, i + by) for i in range(peers) if 0 <= i + by < peers]
    return lax.ppermute(x, axis, pairs)


def transposed_dot(left, right):
    return lax.dot_general(
        left, right, (((0,), (0,)), ((), ())), preferred_element_type=jnp.float32
    )


def ring_neighbours(g, d, groups, peers):
    spot = g * peers + d
    after = lax.rem(spot + 1, groups * peers)
    before = lax.rem(spot + groups * peers - 1, groups * peers)
    following = (after // peers, lax.rem(after, peers))
    previous = (before // peers, lax.rem(before, peers))
    return spot, following, previous


def prepare_kernel(
    groups, peers, basis_ref, tangents_ref, rim_ref, laid_ref, flat, spread, sems
):
    g, d = lax.axis_index("grp"), lax.axis_index("dom")
    spot, following, previous = ring_neighbours(g, d, groups, peers)
    has_next, has_previous = spot < groups * peers - 1, spot > 0
    rim_rows = rim_ref.shape[0]
    elems, width = flat.shape
    lines = width // LANES
    load = pltpu.make_async_copy(tangents_ref, flat, sems.at[0])
    load.start()
    barrier = pltpu.get_barrier_semaphore()
    for present, device in ((has_next, following), (has_previous, previous)):
        @pl.when(present)
        def _(device=device):
            pl.semaphore_signal(barrier, inc=1, device_id=device, device_id_type=MESH)
    pl.semaphore_wait(barrier, has_next.astype(jnp.int32) + has_previous.astype(jnp.int32))
    rim_copy = pltpu.make_async_remote_copy(
        src_ref=basis_ref.at[pl.ds(0, rim_rows)], dst_ref=rim_ref,
        send_sem=sems.at[1], recv_sem=sems.at[2], device_id=previous, device_id_type=MESH,
    )
    pl.when(has_previous)(rim_copy.start)
    load.wait()
    for m in range(lines):
        block = flat[:, m * LANES:(m + 1) * LANES].astype(jnp.float32)
        spread[pl.ds(m, elems, stride=lines + 8), :] = block
    for e in range(elems):
        piece = spread[e * (lines + 8):e * (lines + 8) + lines, :]
        laid_ref[e * lines:(e + 1) * lines, :] = piece.astype(jnp.bfloat16)
    pl.when(has_next)(rim_copy.wait_recv)

    @pl.when(jnp.logical_not(has_next))
    def _():
        rim_ref[...] = jnp.zeros(rim_ref.shape, rim_ref.dtype)

    pl.when(has_previous)(rim_copy.wait_send)


def prepare(basis, tangents, rim_rows, groups, peers):
    elems, width = tangents.shape
    columns = basis.shape[1]
    lines = width // LANES
    vmem = pl.BlockSpec(memory_space=pltpu.VMEM)
    whole = pl.BlockSpec(memory_space=pltpu.HBM)
    return pl.pallas_call(
        functools.partial(prepare_kernel, groups, peers),
        out_shape=(
            jax.ShapeDtypeStruct((rim_rows, columns), jnp.bfloat16),
            jax.ShapeDtypeStruct((elems * lines, LANES), jnp.bfloat16),
        ),
        in_specs=[whole, whole],
        out_specs=(vmem, vmem),
        scratch_shapes=[
            pltpu.VMEM((elems, width), jnp.bfloat16),
            pltpu.VMEM((elems * (lines + 8), LANES), jnp.float32),
            pltpu.SemaphoreType.DMA((3,)),
        ],
        compiler_params=pltpu.CompilerParams(
            collective_id=1, has_side_effects=True, vmem_limit_bytes=VMEM_LIMIT
        ),
        name="prepare",
    )(basis, tangents)


def assemble_kernel(
    own_rows, rim_rows, nodes_ref, weights_ref, basis_hbm, rim_ref, laid_ref,
    rows_ref, edge_ref, over_ref, basis_ref, basis_sem, *scratch,
):
    halves = basis_ref.shape[1] // LANES
    taken = iter(scratch)

    def buffers():
        return [next(taken) for _ in range(halves)]

    table = buffers()
    totals = [buffers() for _ in range(GROUP)]
    picked = [[buffers() for _ in range(GROUP)] for _ in range(2)]
    products = [[buffers() for _ in range(GROUP)] for _ in range(2)]
    node_count, elem_count = nodes_ref.shape
    lines = laid_ref.shape[0] // elem_count
    chunk = rim_rows
    all_rows = own_rows + rim_rows
    load = pltpu.make_async_copy(basis_hbm, basis_ref, basis_sem)
    load.start()

    def clear(i, carry):
        at_rows = pl.ds(pl.multiple_of(i * chunk, chunk), chunk)
        for h in range(halves):
            for u in range(GROUP):
                totals[u][h][at_rows, :] = jnp.zeros((chunk, LANES), jnp.float32)
        return carry

    lax.fori_loop(0, all_rows // chunk, clear, 0)
    for h in range(halves):
        table[h][own_rows:all_rows, :] = rim_ref[:, h * LANES:(h + 1) * LANES].astype(jnp.float32)
        table[h][all_rows:all_rows + 8, :] = jnp.zeros((8, LANES), jnp.float32)
        for u in range(GROUP):
            totals[u][h][all_rows:all_rows + 8, :] = jnp.zeros((8, LANES), jnp.float32)
            for turn in range(2):
                for buffer in (picked[turn][u][h], products[turn][u][h]):
                    buffer[...] = jnp.zeros(buffer.shape, jnp.float32)
    load.wait()

    def widen(i, carry):
        at_rows = pl.ds(pl.multiple_of(i * chunk, chunk), chunk)
        for h in range(halves):
            table[h][at_rows, :] = basis_ref[at_rows, h * LANES:(h + 1) * LANES].astype(jnp.float32)
        return carry

    lax.fori_loop(0, own_rows // chunk, widen, 0)
    keep = lax.broadcasted_iota(jnp.int32, (8, LANES), 0) < 3
    zero = jnp.minimum(nodes_ref[0, 0], 0)

    def scatter(turn, base):
        for k in range(node_count):
            for u in range(GROUP):
                spot = pl.ds(nodes_ref[k, base + u] * 3, 8)
                for h in range(halves):
                    part = jnp.where(keep, products[turn][u][h][pl.ds(zero + 3 * k, 8), :], 0.0)
                    totals[u][h][spot, :] = totals[u][h][spot, :] + part

    def multiply(turn, base):
        for u in range(GROUP):
            for k in range(node_count):
                spot = pl.ds(nodes_ref[k, base + u] * 3, 8)
                for h in range(halves):
                    picked[turn][u][h][pl.ds(zero + 3 * k, 8), :] = table[h][spot, :]
        for u in range(GROUP):
            block = jnp.concatenate([picked[turn][u][h][:EDOF, :] for h in range(halves)], axis=1)
            pairs = laid_ref[pl.ds(pl.multiple_of((base + u) * lines, lines), lines), :]
            matrix = jnp.concatenate([pairs[:, :EDOF], pairs[:, EDOF:]], axis=0)
            product = jnp.dot(
                matrix, block.astype(jnp.bfloat16), preferred_element_type=jnp.float32
            ) * weights_ref[base + u]
            for h in range(halves):
                lanes = slice(h * LANES, (h + 1) * LANES)
                products[turn][u][h][pl.ds(0, lines, stride=2), :] = product[:lines, lanes]
                products[turn][u][h][pl.ds(1, lines, stride=2), :] = product[lines:, lanes]

    def add_pair(i, carry):
        base = i * (2 * GROUP)
        multiply(0, base)
        scatter(1, jnp.maximum(base - GROUP, 0))
        multiply(1, base + GROUP)
        scatter(0, base)
        return carry

    lax.fori_loop(0, elem_count // (2 * GROUP), add_pair, 0)
    scatter(1, elem_count - GROUP)

    def summed(at_rows, h):
        value = totals[0][h][at_rows, :]
        for u in range(1, GROUP):
            value = value + totals[u][h][at_rows, :]
        return value

    def finish(i, carry):
        at_rows = pl.ds(pl.multiple_of(i * chunk, chunk), chunk)
        for h in range(halves):
            rows_ref[at_rows, h * LANES:(h + 1) * LANES] = summed(at_rows, h).astype(jnp.bfloat16)
        return carry

    lax.fori_loop(1, own_rows // chunk, finish, 0)
    for h in range(halves):
        lanes = slice(h * LANES, (h + 1) * LANES)
        edge = summed(pl.ds(0, rim_rows), h)
        edge_ref[:, lanes] = edge
        rows_ref[0:rim_rows, lanes] = edge.astype(jnp.bfloat16)
        over = summed(pl.ds(own_rows, rim_rows), h)
        over_ref[:, lanes] = (over * (1.0 / RIM_SCALE)).astype(over_ref.dtype)


def assemble(basis, rim_basis, laid, nodes, weights):
    own_rows, columns = basis.shape
    rim_rows = rim_basis.shape[0]
    halves = columns // LANES
    tall = pltpu.VMEM((own_rows + rim_rows + 8, LANES), jnp.float32)
    short = pltpu.VMEM((EDOF + 8, LANES), jnp.float32)
    vmem = pl.BlockSpec(memory_space=pltpu.VMEM)
    smem = pl.BlockSpec(memory_space=pltpu.SMEM)
    whole = pl.BlockSpec(memory_space=pltpu.HBM)
    return pl.pallas_call(
        functools.partial(assemble_kernel, own_rows, rim_rows),
        out_shape=(
            jax.ShapeDtypeStruct((own_rows, columns), jnp.bfloat16),
            jax.ShapeDtypeStruct((rim_rows, columns), jnp.float32),
            jax.ShapeDtypeStruct((rim_rows, columns), RIM_TYPE),
        ),
        in_specs=[smem, smem, whole, vmem, vmem],
        out_specs=(vmem, vmem, vmem),
        scratch_shapes=[pltpu.VMEM((own_rows, columns), jnp.bfloat16), pltpu.SemaphoreType.DMA]
        + [tall] * (halves * (1 + GROUP)) + [short] * (halves * GROUP * 4),
        compiler_params=pltpu.CompilerParams(vmem_limit_bytes=VMEM_LIMIT),
        name="assemble",
    )(nodes, weights, basis, rim_basis, laid)


def reduce_kernel(
    peers, factor, basis_hbm, rows_hbm, edge_ref, over_ref, out_ref, edge_out_ref,
    basis_ref, rows_ref, load_sems, arrived, wide, part, half, shards, mine, rim_sems, pair_sems, send_sems, recv_sems,
    spread_sems, spread_recv, pass_sems, pass_recv,
):
    g = lax.axis_index("grp")
    d = lax.axis_index("dom")
    sibling = (1 - g, d)
    rim_rows, columns = edge_ref.shape
    own_rows = basis_ref.shape[0]
    height = columns // peers
    spot, following, previous = ring_neighbours(g, d, 2, peers)
    has_next, has_previous = spot < 2 * peers - 1, spot > 0
    loads = [
        pltpu.make_async_copy(basis_hbm, basis_ref, load_sems.at[0]),
        pltpu.make_async_copy(rows_hbm, rows_ref, load_sems.at[1]),
    ]
    for load in loads:
        load.start()

    def shard(of):
        return pl.ds(pl.multiple_of(of * height, height), height)

    def peer(k):
        return lax.rem(d + k, peers)

    barrier = pltpu.get_barrier_semaphore()
    greeted = [sibling] + [(g, peer(k)) for k in range(1, peers)]
    for device in greeted:
        pl.semaphore_signal(barrier, inc=1, device_id=device, device_id_type=MESH)
    for present, device in ((has_next, following), (has_previous, previous)):
        @pl.when(present)
        def _(device=device):
            pl.semaphore_signal(barrier, inc=1, device_id=device, device_id_type=MESH)
    ring = has_next.astype(jnp.int32) + has_previous.astype(jnp.int32)
    pl.semaphore_wait(barrier, len(greeted) + ring)

    def remote(src, dst, send, recv, device):
        return pltpu.make_async_remote_copy(
            src_ref=src, dst_ref=dst, send_sem=send, recv_sem=recv,
            device_id=device, device_id_type=MESH,
        )

    rim_copy = remote(over_ref, arrived, rim_sems.at[0], rim_sems.at[1], following)
    pl.when(has_next)(rim_copy.start)
    wide[...] = jnp.zeros(wide.shape, jnp.float32)
    for load in loads:
        load.wait()

    def project(i, carry):
        at_rows = pl.ds(pl.multiple_of(i * rim_rows, rim_rows), rim_rows)
        rows = rows_ref[at_rows, :]
        wide[...] += transposed_dot(rows, jnp.concatenate([basis_ref[at_rows, :], rows], axis=1))
        return carry

    lax.fori_loop(1, own_rows // rim_rows, project, 0)
    pl.when(has_previous)(rim_copy.wait_recv)

    @pl.when(jnp.logical_not(has_previous))
    def _():
        arrived[...] = jnp.zeros(arrived.shape, arrived.dtype)

    incoming = arrived[...].astype(jnp.float32) * RIM_SCALE
    edge_rows = (edge_ref[...] + incoming).astype(jnp.bfloat16)
    edge_out_ref[...] = edge_rows
    wide[...] += transposed_dot(
        edge_rows, jnp.concatenate([basis_ref[0:rim_rows, :], edge_rows], axis=1)
    )
    part[0] = wide[:, :columns].T
    part[1] = wide[:, columns:]

    pair_copy = remote(part.at[1 - g], half, pair_sems.at[0], pair_sems.at[1], sibling)
    pair_copy.start()
    pl.when(has_next)(rim_copy.wait_send)
    pair_copy.wait()
    half[...] = half[...] + part[g]

    copies = []
    for k in range(1, peers):
        copy = remote(
            half.at[shard(peer(k))], shards.at[k], send_sems.at[k], recv_sems.at[k], (g, peer(k))
        )
        copy.start()
        copies.append(copy)
    total = half[shard(d), :]
    for k in range(1, peers):
        copies[k - 1].wait_recv()
        total = total + shards[k]
    mine[...] = total * factor
    for copy in copies:
        copy.wait_send()

    spreads = []
    for k in range(1, peers):
        copy = remote(
            mine, out_ref.at[g, shard(d)], spread_sems.at[k], spread_recv.at[k], (g, peer(k))
        )
        copy.start()
        spreads.append(copy)
    passes = []
    own = remote(mine, out_ref.at[g, shard(d)], pass_sems.at[0], pass_recv.at[0], sibling)
    own.start()
    passes.append(own)
    out_ref[g, shard(d), :] = mine[...]
    for k in range(1, peers):
        spreads[k - 1].wait_recv()
        source = lax.rem(d + peers - k, peers)
        place = out_ref.at[g, shard(source)]
        copy = remote(place, place, pass_sems.at[k], pass_recv.at[k], sibling)
        copy.start()
        passes.append(copy)
    for copy in spreads:
        copy.wait_send()
    for copy in passes:
        copy.wait()


def reduce_all(basis, rows, edge, over, peers, factor):
    rim_rows, columns = edge.shape
    height = columns // peers
    vmem = pl.BlockSpec(memory_space=pltpu.VMEM)
    whole = pl.BlockSpec(memory_space=pltpu.HBM)
    dma = pltpu.SemaphoreType.DMA
    return pl.pallas_call(
        functools.partial(reduce_kernel, peers, factor),
        out_shape=(
            jax.ShapeDtypeStruct((2, columns, columns), jnp.float32),
            jax.ShapeDtypeStruct((rim_rows, columns), jnp.bfloat16),
        ),
        in_specs=[whole, whole, vmem, vmem],
        out_specs=(vmem, vmem),
        scratch_shapes=[
            pltpu.VMEM(basis.shape, jnp.bfloat16), pltpu.VMEM(rows.shape, jnp.bfloat16), dma((2,)),
            pltpu.VMEM((rim_rows, columns), RIM_TYPE),
            pltpu.VMEM((columns, 2 * columns), jnp.float32),
            pltpu.VMEM((2, columns, columns), jnp.float32),
            pltpu.VMEM((columns, columns), jnp.float32),
            pltpu.VMEM((peers, height, columns), jnp.float32),
            pltpu.VMEM((height, columns), jnp.float32),
            dma((2,)), dma((2,)), dma((peers,)), dma((peers,)),
            dma((peers,)), dma((peers,)), dma((peers,)), dma((peers,)),
        ],
        compiler_params=pltpu.CompilerParams(
            collective_id=0, has_side_effects=True, vmem_limit_bytes=VMEM_LIMIT
        ),
        name="reduce_all",
    )(basis, rows, edge, over)


def local(reduced_basis, tangents, connectivity, weights):
    own_rows, columns = reduced_basis.shape
    rim_rows = RIM * 3
    groups, peers = lax.axis_size("grp"), lax.axis_size("dom")
    factor = 1.0 / float(own_rows * groups * peers)
    rim_basis, laid = prepare(reduced_basis, tangents, rim_rows, groups, peers)
    rows, edge, over = assemble(reduced_basis, rim_basis, laid, connectivity, weights)
    if groups == 2 and columns % peers == 0 and (columns // peers) % 8 == 0:
        both, edge_rows = reduce_all(reduced_basis, rows, edge, over, peers, factor)
        return lax.dynamic_update_slice(rows, edge_rows, (0, 0)), both[0], both[1]
    incoming = passed_along(over, ("grp", "dom"), 1).astype(jnp.float32) * RIM_SCALE
    edge_rows = (edge + incoming).astype(jnp.bfloat16)
    rows = lax.dynamic_update_slice(rows, edge_rows, (0, 0))
    sums = lax.psum(
        (transposed_dot(reduced_basis, rows), transposed_dot(rows, rows)), ("grp", "dom")
    )
    return rows, sums[0] * factor, sums[1] * factor


def solution(mesh):
    placed = (
        P(("grp", "dom"), None),
        P(("grp", "dom"), None),
        P(None, ("grp", "dom")),
        P(("grp", "dom")),
    )
    return jax.shard_map(
        local,
        mesh=mesh,
        in_specs=placed,
        out_specs=(P(("grp", "dom"), None), P(), P()),
        check_vma=False,
    )
```
